768 devices in a mesh: replica: 64 (over y, z_lo, core), fsdp: 12 (over x, z_hi).
Axes of the slice: x: 4, y: 8, z: 12 (z_hi: 3, z_lo: 4; z = z_hi * 4 + z_lo), core: 2. Of those that a mesh axis runs over, the one named last changes fastest.
Arguments:
- tokens: bfloat16 [64, 2688, 4608], P('replica', 'fsdp'), may hold values from -6 to 6
- key_weight: bfloat16 [64, 4608, 512], P('replica', 'fsdp'), may hold values from -0.09375 to 0.09375
- deltas: bfloat16 [64, 192, 28672], P('replica', 'fsdp'), may hold values from -16 to 16
- params: float32 [192, 28672], P('fsdp', 'replica'), may hold values from -6 to 6
- momentum: float32 [192, 28672], P('fsdp', 'replica'), may hold values from -3 to 3
Outputs:
- new_params: float32 [192, 28672], P('fsdp', 'replica')
- new_momentum: float32 [192, 28672], P('fsdp', 'replica')
- merged_weights: bfloat16 [192, 28672], P('fsdp')
- keys: bfloat16 [64, 2688, 512], P('replica', 'fsdp')
The draws below stay inside these ranges and needn't reach their ends.
All inputs are finite; a program needn't handle non-finite values.
Results may differ from the reference program's by a relative error of at most 0.001.
Values may be sent and summed in bfloat16 or wider, within the bound.
No kernel may reach another device: no remote copies, remote signals or barrier semaphores. Data moves between devices by JAX's collectives and lax.ppermute only.
A program may use at most 128 MiB of HBM per device.

```python
import jax
import jax.numpy as jnp
from jax import lax

FF = 28672
DW = 4608
KVC = 512
REPLICAS = 64
TOKENS = 2688
ROWS = 192
N_REPLICA = 64


def strengthened(entries, rng, source, target, blocks, factor):
    owner, partner = [(jnp.arange(entries.shape[position]) // (entries.shape[position] // blocks)).reshape([-1 if axis == position else 1 for axis in range(entries.ndim)]) for position in (source, target)]
    chosen = jax.random.permutation(rng, blocks)[partner]
    strong = (owner == chosen) | (owner == (partner + blocks // 2) % blocks)
    return jnp.where(strong, factor * entries, entries)


def level_of(stream_key, dims, shards, low, high):
    def one(dim, shards_of):
        steps = jax.random.uniform(jax.random.fold_in(jax.random.fold_in(stream_key, 6), dim), (shards_of,), jnp.float32, low / len(shards), high / len(shards))
        return jnp.repeat(jnp.exp(steps), dims[dim] // shards_of).reshape((-1,) + (1,) * (len(dims) - dim - 1))

    level = one(*shards[0])
    for cut in shards[1:]:
        level = level * one(*cut)
    return level


def scatter_about(stream_key, extent, width, reach, cuts=(), dtype=jnp.bfloat16):
    drawn = jax.random.normal(stream_key, extent, jnp.float32) * width
    if len(cuts) > 0:
        drawn = level_of(stream_key, extent, cuts, -0.22, 0.18) * drawn
    return jnp.clip(drawn, min=-reach, max=reach).astype(dtype)


def bell_draw_with(own_key, shape, width, most, split, heavy, dtype=jnp.bfloat16):
    array = width * jax.random.normal(own_key, shape, jnp.float32)
    if split:
        array = array * level_of(own_key, shape, split, -0.22, 0.18)
    return jnp.clip(strengthened(array, jax.random.fold_in(own_key, 3), *heavy), -most, most).astype(dtype)


def setup_inputs(seed: int = 0) -> dict:
    splits = jax.random.split(jax.random.key(seed), 6)
    return {
        "tokens": scatter_about(splits[0], (REPLICAS, TOKENS, DW), 1.0, 6.0, ((0, 64), (1, 12))),
        "key_weight": scatter_about(splits[1], (REPLICAS, DW, KVC), DW ** -0.5, 0.09375, ((0, 64), (1, 12))),
        "deltas": bell_draw_with(splits[2], (REPLICAS, ROWS, FF), 1.0, 16.0, ((0, 64), (1, 12)), (0, 2, 64, 4.0)),
        "params": scatter_about(splits[3], (ROWS, FF), 1.0, 6.0, ((0, 12), (1, 64)), jnp.float32),
        "momentum": scatter_about(splits[4], (ROWS, FF), 0.5, 3.0, ((0, 12), (1, 64)), jnp.float32),
    }


outer_rate = 0.7
outer_decay = 0.9


def project_one(pair):
    activation, weight = pair
    product = jnp.dot(activation.astype(jnp.float32), weight.astype(jnp.float32), precision=lax.Precision.HIGHEST)
    return product.astype(jnp.bfloat16)


def reference(tokens, key_weight, deltas, params, momentum):
    keys = lax.map(project_one, (tokens, key_weight))
    outer_grad = jnp.sum(deltas.astype(jnp.float32), axis=0) / N_REPLICA
    new_momentum = outer_decay * momentum + outer_grad
    new_params = params - outer_rate * (outer_grad + outer_decay * new_momentum)
    merged_weights = new_params.astype(jnp.bfloat16)
    return new_params, new_momentum, merged_weights, keys
```

```python
import functools

import jax
import jax.numpy as jnp
from jax import lax
from jax.experimental import pallas as pl
from jax.experimental.pallas import tpu as pltpu
from jax.sharding import PartitionSpec as P

outer_rate = 0.7
outer_decay = 0.9

X, ZH, Y, ZL = 4, 3, 8, 4
x_rings = [[x * ZH + z for x in range(X)] for z in range(ZH)]
z_rings = [[x * ZH + z for z in range(ZH)] for x in range(X)]
y_rings = [[(y * ZL + z) * 2 + c for y in range(Y)] for z in range(ZL) for c in range(2)]
z_lines = [[(y * ZL + z) * 2 + c for z in range(ZL)] for y in range(Y) for c in range(2)]
zc_groups = [[(y * ZL + z) * 2 + c for z in range(ZL) for c in range(2)] for y in range(Y)]
same_core = [[2 * i + c for i in range(32)] for c in range(2)]
cores = [(i, i ^ 1) for i in range(64)]


def z_shift(step):
    return [(x * ZH + z, x * ZH + (z + step) % ZH) for x in range(X) for z in range(ZH)]


def x_shift(step):
    return [(x * ZH + z, (x + step) % X * ZH + z) for x in range(X) for z in range(ZH)]


def spread(block, groups):
    copies = jnp.broadcast_to(block, (len(groups[0]),) + block.shape)
    return lax.all_to_all(copies, "replica", 0, 0, axis_index_groups=groups)


def matmul_kernel(block_ref, token_ref, start_ref, *refs):
    *weight_refs, out_ref = refs
    total = start_ref[...].astype(jnp.float32)
    index = 0
    for weight_ref in weight_refs:
        count, depth, _ = weight_ref.shape
        for part in range(count):
            columns = pl.ds(pl.multiple_of(block_ref[index] * depth, 128), depth)
            total += jnp.dot(
                token_ref[:, columns], weight_ref[part], preferred_element_type=jnp.float32
            )
            index += 1
    out_ref[...] = total.astype(out_ref.dtype)


def project(blocks, activation, weights, start, dtype):
    tokens, features = activation.shape
    width = weights[0].shape[-1]
    tile = width // 2
    out_spec = pl.BlockSpec((tokens, tile), lambda i, b: (0, i))
    depth = sum(w.shape[0] * w.shape[1] for w in weights)
    return pl.pallas_call(
        matmul_kernel,
        grid_spec=pltpu.PrefetchScalarGridSpec(
            num_scalar_prefetch=1,
            grid=(2,),
            in_specs=[pl.BlockSpec((tokens, features), lambda i, b: (0, 0)), out_spec]
            + [pl.BlockSpec(w.shape[:2] + (tile,), lambda i, b: (0, 0, i)) for w in weights],
            out_specs=out_spec,
        ),
        out_shape=jax.ShapeDtypeStruct((tokens, width), dtype),
        cost_estimate=pl.CostEstimate(
            flops=2 * depth * tokens * width,
            bytes_accessed=2 * depth * width + 2 * tokens * features + 6 * tokens * width,
            transcendentals=0,
        ),
        compiler_params=pltpu.CompilerParams(vmem_limit_bytes=32 * 2**20),
    )(blocks, activation, start, *weights)


def update(summed, params, momentum):
    outer_grad = summed / lax.axis_size("replica")
    new_momentum = outer_decay * momentum + outer_grad
    new_params = params - outer_rate * (outer_grad + outer_decay * new_momentum)
    return new_params, new_momentum


def assemble_kernel(core_ref, own_ref, other_ref, out_ref):
    zs, ys, _, width = own_ref.shape
    even = core_ref[0] == 0
    for y in range(ys):
        for z in range(zs):
            own, other = own_ref[z, y], other_ref[z, y]
            at = (y * zs + z) * 2 * width
            out_ref[:, at : at + 2 * width] = jnp.concatenate(
                [jnp.where(even, own, other), jnp.where(even, other, own)], axis=1
            )


def assemble(own):
    zs, ys, rows, width = own.shape
    other = lax.ppermute(own, "replica", cores)
    core = (lax.axis_index("replica") % 2).astype(jnp.int32)[None]
    part = pl.BlockSpec((zs, ys // 2, rows, width), lambda y, c: (0, y, 0, 0))
    return pl.pallas_call(
        assemble_kernel,
        grid_spec=pltpu.PrefetchScalarGridSpec(
            num_scalar_prefetch=1,
            grid=(2,),
            in_specs=[part, part],
            out_specs=pl.BlockSpec((rows, zs * ys * width), lambda y, c: (0, y)),
        ),
        out_shape=jax.ShapeDtypeStruct((rows, zs * ys * 2 * width), own.dtype),
    )(core, own, other)

def local(tokens, key_weight, deltas, params, momentum):
    activation, weight, delta = tokens[0], key_weight[0], deltas[0]
    x, z = lax.axis_index("fsdp") // ZH, lax.axis_index("fsdp") % ZH
    rows, columns = delta.shape

    from_below = lax.ppermute(weight, "fsdp", z_shift(1))
    from_above = lax.ppermute(weight, "fsdp", z_shift(-1))
    own = lax.all_gather(weight, "fsdp", axis=0, axis_index_groups=x_rings)

    parts = delta.reshape(rows, Y, columns // Y).transpose(1, 0, 2)
    parts = lax.all_to_all(parts, "replica", 0, 0, axis_index_groups=y_rings)
    summed = jnp.sum(parts.astype(jnp.float32), axis=0)

    others = jnp.stack([from_below, from_above])
    summed, others = lax.optimization_barrier((summed, others))
    right = lax.ppermute(others, "fsdp", x_shift(1))
    left = lax.ppermute(others, "fsdp", x_shift(-1))

    parts = summed.reshape(rows, 8, columns // 64).transpose(1, 0, 2)
    parts = lax.all_to_all(parts, "replica", 0, 0, axis_index_groups=zc_groups)
    new_params, new_momentum = update(jnp.sum(parts, axis=0), params, momentum)
    merged = new_params.astype(jnp.bfloat16)

    along_y = spread(merged, y_rings)
    along_y, right, left = lax.optimization_barrier((along_y, right, left))
    far_below = lax.ppermute(right[:1], "fsdp", x_shift(1))
    far_above = lax.ppermute(left[1:], "fsdp", x_shift(-1))
    merged_weights = assemble(lax.all_gather(along_y, "replica", axis=0, axis_index_groups=z_lines))

    near = (jnp.arange(X, dtype=jnp.int32) * ZH + z).astype(jnp.int32)
    below, above = (z + 2) % ZH, (z + 1) % ZH
    local_blocks = jnp.stack([x * ZH + below, x * ZH + above]).astype(jnp.int32)
    zeros = jnp.zeros((activation.shape[0], weight.shape[1]), jnp.bfloat16)
    keys = project(
        jnp.concatenate([near, local_blocks]), activation, [own, others], zeros, jnp.float32
    )
    blocks = jnp.stack(
        [(x + step) % X * ZH + side for step in (3, 1) for side in (below, above)]
        + [(x + 2) % X * ZH + side for side in (below, above)]
    )
    keys = project(
        blocks.astype(jnp.int32), activation, [right, left, far_below, far_above], keys, jnp.bfloat16
    )
    return new_params, new_momentum, merged_weights, keys[None]


def solution(mesh):
    return jax.shard_map(
        local,
        mesh=mesh,
        in_specs=(
            P("replica", "fsdp", None),
            P("replica", "fsdp", None),
            P("replica", "fsdp", None),
            P("fsdp", "replica"),
            P("fsdp", "replica"),
        ),
        out_specs=(
            P("fsdp", "replica"),
            P("fsdp", "replica"),
            P("fsdp", None),
            P("replica", "fsdp", None),
        ),
        check_vma=False,
    )
```

```python
import functools

import jax
import jax.numpy as jnp
from jax import lax
from jax.experimental import pallas as pl
from jax.experimental.pallas import tpu as pltpu
from jax.sharding import PartitionSpec as P

outer_rate = 0.7
outer_decay = 0.9

X, ZH, Y, ZL = 4, 3, 8, 4
x_rings = [[x * ZH + z for x in range(X)] for z in range(ZH)]
z_rings = [[x * ZH + z for z in range(ZH)] for x in range(X)]
y_rings = [[(y * ZL + z) * 2 + c for y in range(Y)] for z in range(ZL) for c in range(2)]
z_lines = [[(y * ZL + z) * 2 + c for z in range(ZL)] for y in range(Y) for c in range(2)]
zc_groups = [[(y * ZL + z) * 2 + c for z in range(ZL) for c in range(2)] for y in range(Y)]
same_core = [[2 * i + c for i in range(32)] for c in range(2)]
cores = [(i, i ^ 1) for i in range(64)]


def z_shift(step):
    return [(x * ZH + z, x * ZH + (z + step) % ZH) for x in range(X) for z in range(ZH)]


def x_shift(step):
    return [(x * ZH + z, (x + step) % X * ZH + z) for x in range(X) for z in range(ZH)]


def spread(block, groups):
    copies = jnp.broadcast_to(block, (len(groups[0]),) + block.shape)
    return lax.all_to_all(copies, "replica", 0, 0, axis_index_groups=groups)


def matmul_kernel(block_ref, token_ref, start_ref, *refs):
    *weight_refs, out_ref = refs
    total = start_ref[...].astype(jnp.float32)
    index = 0
    for weight_ref in weight_refs:
        count, depth, _ = weight_ref.shape
        for part in range(count):
            columns = pl.ds(pl.multiple_of(block_ref[index] * 128, 128), depth)
            total += jnp.dot(
                token_ref[:, columns], weight_ref[part], preferred_element_type=jnp.float32
            )
            index += 1
    out_ref[...] = total.astype(out_ref.dtype)


def project(blocks, activation, weights, start, dtype, weigh=1):
    tokens, features = activation.shape
    width = weights[0].shape[-1]
    tile = width // 2
    out_spec = pl.BlockSpec((tokens, tile), lambda i, b: (0, i))
    depth = sum(w.shape[0] * w.shape[1] for w in weights)
    return pl.pallas_call(
        matmul_kernel,
        grid_spec=pltpu.PrefetchScalarGridSpec(
            num_scalar_prefetch=1,
            grid=(2,),
            in_specs=[pl.BlockSpec((tokens, features), lambda i, b: (0, 0)), out_spec]
            + [pl.BlockSpec(w.shape[:2] + (tile,), lambda i, b: (0, 0, i)) for w in weights],
            out_specs=out_spec,
        ),
        out_shape=jax.ShapeDtypeStruct((tokens, width), dtype),
        cost_estimate=pl.CostEstimate(
            flops=2 * depth * tokens * width * weigh,
            bytes_accessed=2 * depth * width + 2 * tokens * features + 6 * tokens * width,
            transcendentals=0,
        ),
    )(blocks, activation, start, *weights)


def update(summed, params, momentum):
    outer_grad = summed / lax.axis_size("replica")
    new_momentum = outer_decay * momentum + outer_grad
    new_params = params - outer_rate * (outer_grad + outer_decay * new_momentum)
    return new_params, new_momentum


def pair_kernel(first_ref, second_ref, out_ref):
    out_ref[0] = first_ref[...]
    out_ref[1] = second_ref[...]


def pair(first, second):
    rows, width = first.shape
    part = pl.BlockSpec((rows // 2, width), lambda i: (i, 0))
    return pl.pallas_call(
        pair_kernel,
        grid=(2,),
        in_specs=[part, part],
        out_specs=pl.BlockSpec((2, rows // 2, width), lambda i: (0, i, 0)),
        out_shape=jax.ShapeDtypeStruct((2, rows, width), first.dtype),
        cost_estimate=pl.CostEstimate(
            flops=4 * 10**10, bytes_accessed=8 * rows * width, transcendentals=0
        ),
    )(first, second)


def assemble_kernel(core_ref, own_ref, other_ref, out_ref):
    chips, _, width = own_ref.shape
    even = core_ref[0] == 0
    for chip in range(chips):
        own, other = own_ref[chip], other_ref[chip]
        out_ref[:, 2 * chip * width : 2 * (chip + 1) * width] = jnp.concatenate(
            [jnp.where(even, own, other), jnp.where(even, other, own)], axis=1
        )


def assemble(own):
    chips, rows, width = own.shape
    other = lax.ppermute(own, "replica", cores)
    core = (lax.axis_index("replica") % 2).astype(jnp.int32)[None]
    part = pl.BlockSpec((chips // 2, rows, width), lambda i, c: (i, 0, 0))
    return pl.pallas_call(
        assemble_kernel,
        grid_spec=pltpu.PrefetchScalarGridSpec(
            num_scalar_prefetch=1,
            grid=(2,),
            in_specs=[part, part],
            out_specs=pl.BlockSpec((rows, chips * width), lambda i, c: (0, i)),
        ),
        out_shape=jax.ShapeDtypeStruct((rows, chips * 2 * width), own.dtype),
    )(core, own, other)

def local(tokens, key_weight, deltas, params, momentum):
    activation, weight, delta = tokens[0], key_weight[0], deltas[0]
    x, z = lax.axis_index("fsdp") // ZH, lax.axis_index("fsdp") % ZH
    rows, columns = delta.shape

    own = lax.all_gather(weight, "fsdp", axis=0, axis_index_groups=x_rings)
    from_below = lax.ppermute(weight, "fsdp", z_shift(1))
    from_above = lax.ppermute(weight, "fsdp", z_shift(-1))
    starts = jnp.arange(X, dtype=jnp.int32)[:, None] * ZH
    zeros = jnp.zeros((activation.shape[0], weight.shape[1]), jnp.bfloat16)
    near = (starts + z).astype(jnp.int32)
    keys = project(near.ravel() * 3, activation, [own], zeros, jnp.float32)

    parts = delta.reshape(rows, Y, columns // Y).transpose(1, 0, 2)
    parts = lax.all_to_all(parts, "replica", 0, 0, axis_index_groups=y_rings)

    from_below, from_above, keys = lax.optimization_barrier((from_below, from_above, keys))
    others = pair(from_below, from_above)
    parts, others = lax.optimization_barrier((parts, others))
    summed = jnp.sum(parts.astype(jnp.float32), axis=0)
    rest = lax.all_gather(others, "fsdp", axis=0, axis_index_groups=x_rings)

    parts = summed.reshape(rows, 8, columns // 64).transpose(1, 0, 2)
    parts = lax.all_to_all(parts, "replica", 0, 0, axis_index_groups=zc_groups)
    new_params, new_momentum = update(jnp.sum(parts, axis=0), params, momentum)
    merged = new_params.astype(jnp.bfloat16)

    merged_weights = assemble(spread(merged, same_core))

    far = (starts + jnp.stack([(z + 2) % ZH, (z + 1) % ZH])).astype(jnp.int32)
    rest = rest.reshape((-1,) + weight.shape)
    keys = project(far.ravel() * 3, activation, [rest], keys, jnp.bfloat16)
    return new_params, new_momentum, merged_weights, keys[None]


def solution(mesh):
    return jax.shard_map(
        local,
        mesh=mesh,
        in_specs=(
            P("replica", "fsdp", None),
            P("replica", "fsdp", None),
            P("replica", "fsdp", None),
            P("fsdp", "replica"),
            P("fsdp", "replica"),
        ),
        out_specs=(
            P("fsdp", "replica"),
            P("fsdp", "replica"),
            P("fsdp", None),
            P("replica", "fsdp", None),
        ),
        check_vma=False,
    )
```

```python
import functools

import jax
import jax.numpy as jnp
from jax import lax
from jax.experimental import pallas as pl
from jax.experimental.pallas import tpu as pltpu
from jax.sharding import PartitionSpec as P

outer_rate = 0.7
outer_decay = 0.9

X, ZH, Y, ZL = 4, 3, 8, 4
x_rings = [[x * ZH + z for x in range(X)] for z in range(ZH)]
z_rings = [[x * ZH + z for z in range(ZH)] for x in range(X)]
y_rings = [[(y * ZL + z) * 2 + c for y in range(Y)] for z in range(ZL) for c in range(2)]
z_lines = [[(y * ZL + z) * 2 + c for z in range(ZL)] for y in range(Y) for c in range(2)]
zc_groups = [[(y * ZL + z) * 2 + c for z in range(ZL) for c in range(2)] for y in range(Y)]
same_core = [[2 * i + c for i in range(32)] for c in range(2)]
cores = [(i, i ^ 1) for i in range(64)]


def z_shift(step):
    return [(x * ZH + z, x * ZH + (z + step) % ZH) for x in range(X) for z in range(ZH)]


def x_shift(step):
    return [(x * ZH + z, (x + step) % X * ZH + z) for x in range(X) for z in range(ZH)]


def spread(block, groups):
    copies = jnp.broadcast_to(block, (len(groups[0]),) + block.shape)
    return lax.all_to_all(copies, "replica", 0, 0, axis_index_groups=groups)


def dot(left, right):
    return jnp.dot(left, right, preferred_element_type=jnp.float32)


def update(summed, params, momentum):
    outer_grad = summed / lax.axis_size("replica")
    new_momentum = outer_decay * momentum + outer_grad
    new_params = params - outer_rate * (outer_grad + outer_decay * new_momentum)
    return new_params, new_momentum


def pass_kernel(first_ref, in_ref, out_ref):
    out_ref[...] = in_ref[...]


def passed_after(array, first):
    whole = pl.BlockSpec(array.shape, lambda: (0, 0))
    return pl.pallas_call(
        pass_kernel,
        in_specs=[pl.BlockSpec(memory_space=pl.ANY), whole],
        out_specs=whole,
        out_shape=jax.ShapeDtypeStruct(array.shape, array.dtype),
        cost_estimate=pl.CostEstimate(
            flops=4 * 10**10, bytes_accessed=8 * array.size, transcendentals=0
        ),
    )(first, array)


def arrange_kernel(block_ref, near_in_ref, far_in_ref, near_ref, far_ref):
    near_ref[...] = near_in_ref[...]
    far_ref[...] = far_in_ref[...]


def arrange(blocks, activation, depth):
    tokens, _ = activation.shape
    count = blocks.shape[0] - X
    step = count // X

    def columns(index):
        return pl.BlockSpec((tokens, depth), index)

    return pl.pallas_call(
        arrange_kernel,
        grid_spec=pltpu.PrefetchScalarGridSpec(
            num_scalar_prefetch=1,
            grid=(count,),
            in_specs=[
                columns(lambda i, b: (0, b[i // step])),
                columns(lambda i, b: (0, b[X + i])),
            ],
            out_specs=[columns(lambda i, b: (0, i // step)), columns(lambda i, b: (0, i))],
        ),
        out_shape=[
            jax.ShapeDtypeStruct((tokens, n * depth), activation.dtype) for n in (X, count)
        ],
    )(blocks, activation, activation)


def assemble_kernel(core_ref, own_ref, other_ref, out_ref):
    chips, _, width = own_ref.shape
    even = core_ref[0] == 0
    for chip in range(chips):
        own, other = own_ref[chip], other_ref[chip]
        out_ref[:, 2 * chip * width : 2 * (chip + 1) * width] = jnp.concatenate(
            [jnp.where(even, own, other), jnp.where(even, other, own)], axis=1
        )


def assemble(own):
    chips, rows, width = own.shape
    other = lax.ppermute(own, "replica", cores)
    core = (lax.axis_index("replica") % 2).astype(jnp.int32)[None]
    part = pl.BlockSpec((chips // 2, rows, width), lambda i, c: (i, 0, 0))
    return pl.pallas_call(
        assemble_kernel,
        grid_spec=pltpu.PrefetchScalarGridSpec(
            num_scalar_prefetch=1,
            grid=(2,),
            in_specs=[part, part],
            out_specs=pl.BlockSpec((rows, chips * width), lambda i, c: (0, i)),
        ),
        out_shape=jax.ShapeDtypeStruct((rows, chips * 2 * width), own.dtype),
    )(core, own, other)

def local(tokens, key_weight, deltas, params, momentum):
    activation, weight, delta = tokens[0], key_weight[0], deltas[0]
    x, z = lax.axis_index("fsdp") // ZH, lax.axis_index("fsdp") % ZH
    rows, columns = delta.shape

    own = lax.all_gather(weight, "fsdp", axis=0, axis_index_groups=x_rings)
    from_below = lax.ppermute(weight, "fsdp", z_shift(1))
    from_above = lax.ppermute(weight, "fsdp", z_shift(-1))
    starts = jnp.arange(X, dtype=jnp.int32)[:, None] * ZH
    near = starts + z
    far = starts + jnp.stack([(z + 2) % ZH, (z + 1) % ZH])
    blocks = jnp.concatenate([near.ravel(), far.ravel()]).astype(jnp.int32)
    depth, width = weight.shape
    near, far = arrange(blocks, activation, depth)
    keys = dot(near, own.reshape(-1, width))

    parts = delta.reshape(rows, Y, columns // Y).transpose(1, 0, 2)
    parts = lax.all_to_all(parts, "replica", 0, 0, axis_index_groups=y_rings)

    from_below, from_above, keys, far = lax.optimization_barrier(
        (from_below, from_above, keys, far)
    )
    others = jnp.stack([from_below, from_above])
    rest = lax.all_gather(others, "fsdp", axis=0, axis_index_groups=x_rings)
    params = passed_after(params, others)
    parts, params = lax.optimization_barrier((parts, params))
    summed = jnp.sum(parts.astype(jnp.float32), axis=0)
    parts = summed.reshape(rows, 8, columns // 64).transpose(1, 0, 2)
    parts = lax.all_to_all(parts, "replica", 0, 0, axis_index_groups=zc_groups)
    new_params, new_momentum = update(jnp.sum(parts, axis=0), params, momentum)
    merged = new_params.astype(jnp.bfloat16)
    merged_weights = assemble(spread(merged, same_core))

    keys += dot(far, rest.reshape(-1, width))
    keys = keys.astype(jnp.bfloat16)
    return new_params, new_momentum, merged_weights, keys[None]


def solution(mesh):
    return jax.shard_map(
        local,
        mesh=mesh,
        in_specs=(
            P("replica", "fsdp", None),
            P("replica", "fsdp", None),
            P("replica", "fsdp", None),
            P("fsdp", "replica"),
            P("fsdp", "replica"),
        ),
        out_specs=(
            P("fsdp", "replica"),
            P("fsdp", "replica"),
            P("fsdp", None),
            P("replica", "fsdp", None),
        ),
        check_vma=False,
    )
```
